32 devices in a mesh: grp: 4 (over y, core), pen: 8 (over z, x).
Axes of the slice: x: 2, y: 2, z: 4, core: 2. Of those that a mesh axis runs over, the one named last changes fastest.
Arguments:
- pressure_source: float32 [16, 1024, 4096], P('grp', None, 'pen'), may hold values from -15 to 15
- solid_temp: float32 [16, 1024, 4096], P(None, 'grp', 'pen'), may hold values from -6 to 6
- gas_wall_temp: float32 [1024, 4096], P('grp', 'pen'), may hold values from -6 to 6
- phase_map: int32 [16, 1024, 4096], P(None, 'grp', 'pen'), may hold values 0 or 1
- phase_conductivity: float32 [2], replicated, may hold values from 0.3 to 1
Outputs:
- pressure: float32 [16, 1024, 4096], P('grp', None, 'pen')
- solid_final: float32 [16, 1024, 4096], P(None, 'grp', 'pen')
The draws below stay inside these ranges and needn't reach their ends.
All inputs are finite; a program needn't handle non-finite values. No bound on the sum of `phase_map` on one device may be relied on, other than what follows from the above.
Results may differ from the reference program's by a relative error of at most 0.0003.
Values sent between devices are 32-bit elements; how exact they have to be, the bound alone decides.
A program may use at most 128 MiB of HBM per device.

```python
import math
import jax
import jax.numpy as jnp

NX = 4096
NY = 1024
NZ = 16
SZ = 16
PHASES = 2


def draw_pressure_source(key, part):
    key = jax.random.fold_in(key, 11)
    grid_shape = (NZ, NY, NX)
    return jnp.clip(3.0 * jax.random.normal(key, grid_shape, jnp.float32), -15.0, 15.0)


def plant(drawn, stream_key, least, top_value):
    longest = drawn.shape.index(max(drawn.shape))
    spots = []
    for shift in (0, 1):
        where = [jax.random.randint(jax.random.fold_in(stream_key, axis), (), 0, length) for axis, length in enumerate(drawn.shape)]
        where[longest] = (where[longest] + shift) % drawn.shape[longest]
        spots.append(tuple(where))
    return drawn.at[spots[0]].set(least).at[spots[1]].set(top_value)


def level_of(key, dims, shards, least, top_value):
    gain = 1.0
    for dim, shards_of in shards:
        steps = jax.random.uniform(jax.random.fold_in(jax.random.fold_in(key, 6), dim), (shards_of,), jnp.float32, least / len(shards), top_value / len(shards))
        gain = gain * jnp.repeat(jnp.exp(steps), dims[dim] // shards_of).reshape((-1,) + (1,) * (len(dims) - 1 - dim))
    return gain


def gaussian(stream_key, dims, deviation, reach, pieces=(), kind=jnp.bfloat16):
    drawn = deviation * jax.random.normal(stream_key, dims, jnp.float32)
    if pieces:
        drawn = drawn * level_of(stream_key, dims, pieces, -0.22, 0.18)
    return jnp.clip(drawn, -reach, reach).astype(kind)


def setup_inputs(seed: int = 0) -> dict:
    splits = jax.random.split(jax.random.key(seed), 6)
    pressure_source = draw_pressure_source(jax.random.fold_in(splits[5], 71), 0)
    solid_temp = gaussian(splits[1], (SZ, NY, NX), 1.0, 6.0, ((1, 4), (2, 8)), jnp.float32)
    gas_wall_temp = gaussian(splits[2], (NY, NX), 1.0, 6.0, ((0, 4), (1, 8)), jnp.float32)
    phase_map = plant((jax.random.randint(splits[3], (SZ, NY, NX), 0, 2) < 1).astype(jnp.int32), jax.random.fold_in(splits[3], 1), 0, 1)
    phase_conductivity = jnp.clip(jnp.exp(jax.random.uniform(splits[4], (PHASES,), jnp.float32, math.log(0.3), math.log(1.0))), 0.3, 1.0)
    return {"pressure_source": pressure_source, "solid_temp": solid_temp, "gas_wall_temp": gas_wall_temp, "phase_map": phase_map, "phase_conductivity": phase_conductivity}


HEAT_TRANSFER = 1.0
PRESSURE_WORK = 0.5
STEP_RATE = 0.12


def hartley(field_in, axis_num):
    complex_spec = jnp.fft.fft(field_in, axis=axis_num)
    return jnp.real(complex_spec) - jnp.imag(complex_spec)


def depth_solve(source, eigen_sum):
    depth_len = source.shape[0]
    pivot_now = eigen_sum - 1.0
    carry_now = source[0]
    pivot_list = [pivot_now]
    carry_list = [carry_now]
    for plane_idx in range(1, depth_len):
        inverse = 1.0 / pivot_now
        pivot_now = eigen_sum - 2.0 - inverse
        carry_now = source[plane_idx] - inverse * carry_now
        pivot_list.append(pivot_now)
        carry_list.append(carry_now)
    upper_val = carry_list[depth_len - 1] / pivot_list[depth_len - 1]
    result_rows = [upper_val]
    for plane_idx in range(depth_len - 2, -1, -1):
        upper_val = (carry_list[plane_idx] - upper_val) / pivot_list[plane_idx]
        result_rows.append(upper_val)
    return jnp.stack(result_rows[::-1])


def conduct(padded_temp, padded_cond, flux_src):
    centre_temp = padded_temp[:, 1:-1, 1:-1]
    centre_cond = padded_cond[:, 1:-1, 1:-1]
    net_flux = jnp.zeros_like(centre_temp)
    neighbours = ((padded_temp[:, :-2, 1:-1], padded_cond[:, :-2, 1:-1]),
                  (padded_temp[:, 2:, 1:-1], padded_cond[:, 2:, 1:-1]),
                  (padded_temp[:, 1:-1, :-2], padded_cond[:, 1:-1, :-2]),
                  (padded_temp[:, 1:-1, 2:], padded_cond[:, 1:-1, 2:]))
    for shift_temp, shift_cond in neighbours:
        net_flux = net_flux + 0.5 * (centre_cond + shift_cond) * (shift_temp - centre_temp)
    vertical = 0.5 * (centre_cond[1:] + centre_cond[:-1]) * (centre_temp[1:] - centre_temp[:-1])
    net_flux = net_flux + jnp.pad(vertical, ((0, 1), (0, 0), (0, 0))) - jnp.pad(vertical, ((1, 0), (0, 0), (0, 0)))
    surface = jnp.concatenate([flux_src[None], jnp.zeros_like(centre_temp[1:])], axis=0)
    return centre_temp + STEP_RATE * (net_flux + surface)


def reference(pressure_source, solid_temp, gas_wall_temp, phase_map, phase_conductivity):
    spectrum = hartley(hartley(pressure_source, 1), 2)
    span_wave = jnp.arange(NY, dtype=jnp.float32)
    stream_wave = jnp.arange(NX, dtype=jnp.float32)
    eigen_span = 2.0 * jnp.cos(span_wave * (2.0 * math.pi / NY)) - 2.0
    eigen_stream = 2.0 * jnp.cos(stream_wave * (2.0 * math.pi / NX)) - 2.0
    eigen_sum = eigen_span[:, None] + eigen_stream[None, :]
    solved = depth_solve(spectrum, eigen_sum) * (1.0 / (NX * NY))
    pressure = hartley(hartley(solved, 2), 1)
    surface_flux = HEAT_TRANSFER * (gas_wall_temp + PRESSURE_WORK * pressure[0] - solid_temp[0])
    cell_cond = jnp.where(phase_map == 1, phase_conductivity[1], phase_conductivity[0])
    padded_cond = jnp.pad(cell_cond, ((0, 0), (1, 1), (1, 1)), mode="wrap")
    temp_now = solid_temp
    for section_idx in range(2):
        padded_temp = jnp.pad(temp_now, ((0, 0), (1, 1), (1, 1)), mode="wrap")
        temp_now = conduct(padded_temp, padded_cond, surface_flux)
    return pressure, temp_now
```

```python
import functools
import math

import jax
import jax.numpy as jnp
import numpy as np
from jax import lax
from jax.experimental import pallas as pl
from jax.experimental.pallas import tpu as pltpu
from jax.sharding import PartitionSpec as P

HIGH = lax.Precision.HIGH
HEAT_TRANSFER = 1.0
PRESSURE_WORK = 0.5
STEP_RATE = 0.12
LANES = 128
SEGMENTS = 8
VMEM_BYTES = 56 * 2**20


def params():
    return pltpu.CompilerParams(vmem_limit_bytes=VMEM_BYTES)


def with_halo(cells, sides, width):
    for axis, dim in sides:
        count = lax.axis_size(axis)
        head = lax.slice_in_dim(cells, 0, width, axis=dim)
        tail = lax.slice_in_dim(cells, cells.shape[dim] - width, cells.shape[dim], axis=dim)
        cells = jnp.concatenate(
            [
                lax.ppermute(tail, axis, [(i, (i + 1) % count) for i in range(count)]),
                cells,
                lax.ppermute(head, axis, [((i + 1) % count, i) for i in range(count)]),
            ],
            axis=dim,
        )
    return cells


def cas(product, length):
    angle = (product % length) * (2.0 * math.pi / length)
    return np.cos(angle) + np.sin(angle)


def depth_modes(depth_len):
    matrix = np.diag(np.full(depth_len, -2.0))
    matrix += np.diag(np.ones(depth_len - 1), 1) + np.diag(np.ones(depth_len - 1), -1)
    matrix[0, 0] = -1.0
    values, vectors = np.linalg.eigh(matrix)
    return -values, vectors.T


def wave_order(span_len, groups):
    order = np.concatenate([np.arange(0, span_len, 2), np.arange(1, span_len, 2)])
    return order.reshape(groups, span_len // groups)


def split(value):
    high = value.astype(jnp.bfloat16)
    low = (value - high.astype(jnp.float32)).astype(jnp.bfloat16)
    return high, low


def dot_split(left, right, dims):
    dot = functools.partial(
        lax.dot_general, dimension_numbers=(dims, ((), ())), preferred_element_type=jnp.float32
    )
    return dot(left[0], right[0]) + dot(left[0], right[1]) + dot(left[1], right[0])


def span_forward_kernel(source_ref, table_ref, out_ref):
    half = table_ref.shape[2]
    width = out_ref.shape[3]
    head = source_ref[0, :half]
    tail = source_ref[0, half:]
    for parity in range(2):
        folded = split(head - tail if parity else head + tail)
        table = (table_ref[parity, 0], table_ref[parity, 1])
        result = dot_split(folded, table, ((0,), (0,)))
        per = half // width
        for part in range(per):
            out_ref[parity * per + part, 0] = result[:, part * width : (part + 1) * width]


def span_inverse_kernel(waves_ref, table_ref, out_ref):
    half = table_ref.shape[2]
    per = waves_ref.shape[0] // 2
    halves = []
    for parity in range(2):
        table = (table_ref[parity, 0], table_ref[parity, 1])
        waves = jnp.concatenate([waves_ref[parity * per + part, 0] for part in range(per)], axis=1)
        halves.append(dot_split(table, split(waves), ((1,), (1,))))
    out_ref[0, :half] = halves[0] + halves[1]
    out_ref[0, half:] = halves[0] - halves[1]


def mix(weights, planes):
    result = []
    for row in weights:
        total = float(row[0]) * planes[0]
        for weight, plane in zip(row[1:], planes[1:]):
            total = total + float(weight) * plane
        result.append(total)
    return result


def ends_kernel(vectors, source_ref, root_ref, modes_ref, head_ref, tail_ref):
    depth_len, steps = modes_ref.shape[0], modes_ref.shape[1]

    def ahead(step, carry):
        planes = [
            source_ref[plane, pl.ds(step, SEGMENTS, stride=steps), :] for plane in range(depth_len)
        ]
        made = []
        for mode, value in enumerate(mix(vectors, planes)):
            modes_ref[mode, step] = value
            made.append(value + root_ref[mode][None] * carry[mode])
        return tuple(made)

    def back(step, carry):
        return tuple(
            modes_ref[mode, steps - 1 - step] + root_ref[mode][None] * carry[mode]
            for mode in range(depth_len)
        )

    zero = tuple(jnp.zeros((SEGMENTS, LANES), jnp.float32) for _ in range(depth_len))
    ended = lax.fori_loop(0, steps, ahead, zero)
    for mode in range(depth_len):
        tail_ref[mode] = ended[mode]
    ended = lax.fori_loop(0, steps, back, zero)
    for mode in range(depth_len):
        head_ref[mode] = ended[mode]


def solve_kernel(vectors, modes_ref, root_ref, gain_ref, left_ref, right_ref, out_ref, ahead_ref):
    depth_len, steps = modes_ref.shape[0], modes_ref.shape[1]

    def ahead(step, carry):
        made = []
        for mode in range(depth_len):
            value = modes_ref[mode, step] + root_ref[mode][None] * carry[mode]
            ahead_ref[mode, step] = value
            made.append(value)
        return tuple(made)

    def back(count, carry):
        step = steps - 1 - count
        made, solved = [], []
        for mode in range(depth_len):
            coming = root_ref[mode][None] * carry[mode]
            solved.append(gain_ref[mode][None] * (ahead_ref[mode, step] + coming))
            made.append(modes_ref[mode, step] + coming)
        for plane, value in enumerate(mix(vectors.T, solved)):
            out_ref[plane, pl.ds(step, SEGMENTS, stride=steps), :] = value
        return tuple(made)

    lax.fori_loop(0, steps, ahead, tuple(left_ref[mode] for mode in range(depth_len)))
    lax.fori_loop(0, steps, back, tuple(right_ref[mode] for mode in range(depth_len)))


def conduct(padded_temp, padded_cond):
    centre_temp = padded_temp[:, 1:-1, 1:-1]
    centre_cond = padded_cond[:, 1:-1, 1:-1]
    net_flux = jnp.zeros_like(centre_temp)
    neighbours = (
        (padded_temp[:, :-2, 1:-1], padded_cond[:, :-2, 1:-1]),
        (padded_temp[:, 2:, 1:-1], padded_cond[:, 2:, 1:-1]),
        (padded_temp[:, 1:-1, :-2], padded_cond[:, 1:-1, :-2]),
        (padded_temp[:, 1:-1, 2:], padded_cond[:, 1:-1, 2:]),
    )
    for shift_temp, shift_cond in neighbours:
        net_flux = net_flux + 0.5 * (centre_cond + shift_cond) * (shift_temp - centre_temp)
    if centre_temp.shape[0] > 1:
        vertical = 0.5 * (centre_cond[1:] + centre_cond[:-1]) * (centre_temp[1:] - centre_temp[:-1])
        net_flux = (
            net_flux
            + jnp.pad(vertical, ((0, 1), (0, 0), (0, 0)))
            - jnp.pad(vertical, ((1, 0), (0, 0), (0, 0)))
        )
    return centre_temp + STEP_RATE * net_flux


def per_device(pressure_source, solid_temp, gas_wall_temp, phase_map, phase_conductivity):
    groups = lax.axis_size("grp")
    pencils = lax.axis_size("pen")
    group_idx = lax.axis_index("grp")
    pencil_idx = lax.axis_index("pen")
    depth_loc, span_len, stream_loc = pressure_source.shape
    stream_len = stream_loc * pencils
    depth_len = depth_loc * groups
    half = span_len // 2
    waves_loc = span_len // groups
    steps = stream_loc // SEGMENTS
    f32 = jnp.float32

    order = wave_order(span_len, groups)
    row = np.arange(half)
    table = np.stack([cas(row[:, None] * (2 * row + parity)[None, :], span_len) for parity in (0, 1)])
    table_high = table.astype(jnp.bfloat16)
    table_low = (table - table_high.astype(np.float64)).astype(jnp.bfloat16)
    table_parts = jnp.asarray(np.stack([table_high, table_low], axis=1))
    lambdas, vectors = depth_modes(depth_len)
    eigen_span = 2.0 * np.cos(2.0 * math.pi * order / span_len) - 2.0
    shift = lambdas[None, :, None] - eigen_span[:, None, :]
    root = 2.0 / (shift + 2.0 + np.sqrt(shift * (shift + 4.0)))
    gain = -1.0 / (1.0 / root - root) / span_len
    around = np.arange(pencils)[:, None, None, None]
    reach = np.power(root, stream_loc * around) / (1.0 - np.power(root, stream_len))

    def mine(constant, axis):
        chosen = lax.dynamic_index_in_dim(jnp.asarray(constant, f32), group_idx, axis, keepdims=False)
        return chosen

    root_loc = mine(root, 0)
    gain_loc = mine(gain, 0)
    hop_loc = mine(np.power(root, steps), 0)
    reach_loc = mine(reach, 1)
    falling = jnp.roll(jnp.flip(reach_loc, 0), 1, 0)
    reach_left = lax.dynamic_slice_in_dim(
        jnp.concatenate([falling, falling]), (pencils + 1 - pencil_idx) % pencils, pencils, 0
    )
    reach_right = lax.dynamic_slice_in_dim(
        jnp.concatenate([reach_loc, reach_loc]), (2 * pencils - 1 - pencil_idx) % pencils, pencils, 0
    )

    spectral = pl.pallas_call(
        span_forward_kernel,
        grid=(depth_loc,),
        in_specs=[
            pl.BlockSpec((1, span_len, stream_loc), lambda z: (z, 0, 0)),
            pl.BlockSpec((2, 2, half, half), lambda z: (0, 0, 0, 0)),
        ],
        out_specs=pl.BlockSpec((groups, 1, stream_loc, waves_loc), lambda z: (0, z, 0, 0)),
        out_shape=jax.ShapeDtypeStruct((groups, depth_loc, stream_loc, waves_loc), f32),
        compiler_params=params(),
        cost_estimate=pl.CostEstimate(
            flops=6 * depth_loc * stream_loc * span_len * half,
            bytes_accessed=8 * depth_loc * stream_loc * span_len,
            transcendentals=0,
        ),
        name="span_forward",
    )(pressure_source, table_parts)
    moved = lax.all_to_all(spectral, "grp", split_axis=0, concat_axis=0, tiled=True)
    moved = moved.reshape(depth_len, stream_loc, waves_loc)

    data_spec = pl.BlockSpec((depth_len, stream_loc, LANES), lambda w: (0, 0, w))
    mode_spec = pl.BlockSpec((depth_len, steps, SEGMENTS, LANES), lambda w: (0, 0, 0, w))
    wave_spec = pl.BlockSpec((depth_len, 1, LANES), lambda w: (0, 0, w))
    ends_spec = pl.BlockSpec((depth_len, SEGMENTS, LANES), lambda w: (0, 0, w))
    ends_shape = jax.ShapeDtypeStruct((depth_len, SEGMENTS, waves_loc), f32)
    cost = pl.CostEstimate(
        flops=2 * depth_len**2 * stream_loc * waves_loc,
        bytes_accessed=8 * depth_len * stream_loc * waves_loc,
        transcendentals=0,
    )

    def rowed(value):
        return value[:, None, :]

    modes, heads, tails = pl.pallas_call(
        lambda s, r, m, h, t: ends_kernel(vectors, s, FirstRow(r), m, h, t),
        grid=(waves_loc // LANES,),
        in_specs=[data_spec, wave_spec],
        out_specs=[mode_spec, ends_spec, ends_spec],
        out_shape=[
            jax.ShapeDtypeStruct((depth_len, steps, SEGMENTS, waves_loc), f32),
            ends_shape,
            ends_shape,
        ],
        compiler_params=params(),
        cost_estimate=cost,
        name="stream_ends",
    )(moved, rowed(root_loc))
    tail_all = tails[:, 0]
    head_all = heads[:, SEGMENTS - 1]
    for part in range(1, SEGMENTS):
        tail_all = tails[:, part] + hop_loc * tail_all
        head_all = heads[:, SEGMENTS - 1 - part] + hop_loc * head_all
    gathered = lax.all_gather(jnp.stack([tail_all, head_all]), "pen")
    left = [jnp.sum(reach_left * gathered[:, 0], axis=0)]
    right = [jnp.sum(reach_right * gathered[:, 1], axis=0)]
    for part in range(SEGMENTS - 1):
        left.append(tails[:, part] + hop_loc * left[-1])
        right.append(heads[:, SEGMENTS - 1 - part] + hop_loc * right[-1])
    solved = pl.pallas_call(
        lambda m, r, g, a, b, o, c: solve_kernel(vectors, m, FirstRow(r), FirstRow(g), a, b, o, c),
        grid=(waves_loc // LANES,),
        in_specs=[mode_spec, wave_spec, wave_spec, ends_spec, ends_spec],
        out_specs=data_spec,
        out_shape=jax.ShapeDtypeStruct((depth_len, stream_loc, waves_loc), f32),
        scratch_shapes=[pltpu.VMEM((depth_len, steps, SEGMENTS, LANES), f32)],
        compiler_params=params(),
        cost_estimate=cost,
        name="stream_solve",
    )(modes, rowed(root_loc), rowed(gain_loc), jnp.stack(left, 1), jnp.stack(right[::-1], 1))

    returned = lax.all_to_all(
        solved.reshape(groups, depth_loc, stream_loc, waves_loc),
        "grp",
        split_axis=0,
        concat_axis=0,
        tiled=True,
    )
    pressure = pl.pallas_call(
        span_inverse_kernel,
        grid=(depth_loc,),
        in_specs=[
            pl.BlockSpec((groups, 1, stream_loc, waves_loc), lambda z: (0, z, 0, 0)),
            pl.BlockSpec((2, 2, half, half), lambda z: (0, 0, 0, 0)),
        ],
        out_specs=pl.BlockSpec((1, span_len, stream_loc), lambda z: (z, 0, 0)),
        out_shape=jax.ShapeDtypeStruct((depth_loc, span_len, stream_loc), f32),
        compiler_params=params(),
        cost_estimate=pl.CostEstimate(
            flops=6 * depth_loc * stream_loc * span_len * half,
            bytes_accessed=8 * depth_loc * stream_loc * span_len,
            transcendentals=0,
        ),
        name="span_inverse",
    )(returned, table_parts)

    tile_rows = span_len // groups
    sides = (("grp", 1), ("pen", 2))
    cell_cond = jnp.where(phase_map == 1, phase_conductivity[1], phase_conductivity[0])
    padded_temp, padded_cond = with_halo(solid_temp, sides, 1), with_halo(cell_cond, sides, 1)
    first_temp = conduct(padded_temp, padded_cond)
    unheated = conduct(with_halo(first_temp, sides, 1), padded_cond)
    dry_flux = with_halo((gas_wall_temp - solid_temp[0])[None], sides, 1)

    span_rows = np.arange(-1, span_len + 1) % span_len
    wall_table = cas(span_rows[:, None] * order.reshape(1, -1), span_len)
    wall_rows = lax.dynamic_slice_in_dim(
        jnp.asarray(wall_table, f32), group_idx * tile_rows, tile_rows + 2, 0
    )
    wall_waves = lax.all_gather(solved[0], "grp")
    wall = jnp.einsum(
        "ygk,gxk->yx",
        wall_rows.reshape(tile_rows + 2, groups, waves_loc),
        wall_waves,
        precision=HIGH,
        preferred_element_type=f32,
    )
    wall = with_halo(wall[None], (("pen", 2),), 1)
    flux = HEAT_TRANSFER * (dry_flux + PRESSURE_WORK * wall)
    centre_flux = flux[0, 1:-1, 1:-1]
    between = 0.5 * (padded_cond[0] + padded_cond[1])[1:-1, 1:-1] * centre_flux
    lateral = conduct(flux, padded_cond[:1])[0]
    top = STEP_RATE * (centre_flux + lateral - STEP_RATE * between)
    second = STEP_RATE * STEP_RATE * between
    final_temp = unheated.at[0].add(top).at[1].add(second)
    return (pressure, final_temp)


class FirstRow:
    def __init__(self, ref):
        self.ref = ref

    def __getitem__(self, mode):
        return self.ref[mode, 0]


def solution(mesh):
    in_specs = (
        P("grp", None, "pen"),
        P(None, "grp", "pen"),
        P("grp", "pen"),
        P(None, "grp", "pen"),
        P(),
    )
    out_specs = (P("grp", None, "pen"), P(None, "grp", "pen"))
    return jax.shard_map(
        per_device, mesh=mesh, in_specs=in_specs, out_specs=out_specs, check_vma=False
    )
```

```python
import functools
import math

import jax
import jax.numpy as jnp
import numpy as np
from jax import lax
from jax.experimental import pallas as pl
from jax.experimental.pallas import tpu as pltpu
from jax.sharding import PartitionSpec as P

HIGH = lax.Precision.HIGH
HEAT_TRANSFER = 1.0
PRESSURE_WORK = 0.5
STEP_RATE = 0.12
LANES = 128
SEGMENTS = 8
ROWS = 8
WIDTH = 2
VMEM_BYTES = 56 * 2**20


def params():
    return pltpu.CompilerParams(vmem_limit_bytes=VMEM_BYTES)


def swap_edges(cells, axis, dim, width):
    count = lax.axis_size(axis)
    head = lax.slice_in_dim(cells, 0, width, axis=dim)
    tail = lax.slice_in_dim(cells, cells.shape[dim] - width, cells.shape[dim], axis=dim)
    return (
        lax.ppermute(tail, axis, [(i, (i + 1) % count) for i in range(count)]),
        lax.ppermute(head, axis, [((i + 1) % count, i) for i in range(count)]),
    )


def cas(product, length):
    angle = (product % length) * (2.0 * math.pi / length)
    return np.cos(angle) + np.sin(angle)


def depth_modes(depth_len):
    matrix = np.diag(np.full(depth_len, -2.0))
    matrix += np.diag(np.ones(depth_len - 1), 1) + np.diag(np.ones(depth_len - 1), -1)
    matrix[0, 0] = -1.0
    values, vectors = np.linalg.eigh(matrix)
    return -values, vectors.T


def wave_order(span_len, groups):
    order = np.concatenate([np.arange(0, span_len, 2), np.arange(1, span_len, 2)])
    return order.reshape(groups, span_len // groups)


def split(value):
    high = value.astype(jnp.bfloat16)
    low = (value - high.astype(jnp.float32)).astype(jnp.bfloat16)
    return high, low


def dot_split(left, right, dims):
    dot = functools.partial(
        lax.dot_general, dimension_numbers=(dims, ((), ())), preferred_element_type=jnp.float32
    )
    return dot(left[0], right[0]) + dot(left[0], right[1]) + dot(left[1], right[0])


def span_forward_kernel(source_ref, table_ref, out_ref):
    half = table_ref.shape[2]
    width = out_ref.shape[3]
    head = source_ref[0, :half]
    tail = source_ref[0, half:]
    for parity in range(2):
        folded = split(head - tail if parity else head + tail)
        table = (table_ref[parity, 0], table_ref[parity, 1])
        result = dot_split(folded, table, ((0,), (0,)))
        per = half // width
        for part in range(per):
            out_ref[parity * per + part, 0] = result[:, part * width : (part + 1) * width]


def span_inverse_kernel(waves_ref, table_ref, out_ref):
    half = table_ref.shape[2]
    per = waves_ref.shape[0] // 2
    halves = []
    for parity in range(2):
        table = (table_ref[parity, 0], table_ref[parity, 1])
        waves = jnp.concatenate([waves_ref[parity * per + part, 0] for part in range(per)], axis=1)
        halves.append(dot_split(table, split(waves), ((1,), (1,))))
    out_ref[0, :half] = halves[0] + halves[1]
    out_ref[0, half:] = halves[0] - halves[1]


def mix(weights, planes):
    result = []
    for row in weights:
        total = float(row[0]) * planes[0]
        for weight, plane in zip(row[1:], planes[1:]):
            total = total + float(weight) * plane
        result.append(total)
    return result


def ends_kernel(vectors, source_ref, root_ref, modes_ref, head_ref, tail_ref):
    depth_len, steps = modes_ref.shape[0], modes_ref.shape[1]

    def ahead(step, carry):
        planes = [
            source_ref[plane, pl.ds(step, SEGMENTS, stride=steps), :] for plane in range(depth_len)
        ]
        made = []
        for mode, value in enumerate(mix(vectors, planes)):
            modes_ref[mode, step] = value
            made.append(value + root_ref[mode][None] * carry[mode])
        return tuple(made)

    def back(step, carry):
        return tuple(
            modes_ref[mode, steps - 1 - step] + root_ref[mode][None] * carry[mode]
            for mode in range(depth_len)
        )

    zero = tuple(jnp.zeros((SEGMENTS, LANES), jnp.float32) for _ in range(depth_len))
    ended = lax.fori_loop(0, steps, ahead, zero)
    for mode in range(depth_len):
        tail_ref[mode] = ended[mode]
    ended = lax.fori_loop(0, steps, back, zero)
    for mode in range(depth_len):
        head_ref[mode] = ended[mode]


def solve_kernel(vectors, modes_ref, root_ref, gain_ref, left_ref, right_ref, out_ref, ahead_ref):
    depth_len, steps = modes_ref.shape[0], modes_ref.shape[1]

    def ahead(step, carry):
        made = []
        for mode in range(depth_len):
            value = modes_ref[mode, step] + root_ref[mode][None] * carry[mode]
            ahead_ref[mode, step] = value
            made.append(value)
        return tuple(made)

    def back(count, carry):
        step = steps - 1 - count
        made, solved = [], []
        for mode in range(depth_len):
            coming = root_ref[mode][None] * carry[mode]
            solved.append(gain_ref[mode][None] * (ahead_ref[mode, step] + coming))
            made.append(modes_ref[mode, step] + coming)
        for plane, value in enumerate(mix(vectors.T, solved)):
            out_ref[plane, pl.ds(step, SEGMENTS, stride=steps), :] = value
        return tuple(made)

    lax.fori_loop(0, steps, ahead, tuple(left_ref[mode] for mode in range(depth_len)))
    lax.fori_loop(0, steps, back, tuple(right_ref[mode] for mode in range(depth_len)))


def conduct(padded_temp, padded_cond):
    centre_temp = padded_temp[:, 1:-1, 1:-1]
    centre_cond = padded_cond[:, 1:-1, 1:-1]
    net_flux = jnp.zeros_like(centre_temp)
    neighbours = (
        (padded_temp[:, :-2, 1:-1], padded_cond[:, :-2, 1:-1]),
        (padded_temp[:, 2:, 1:-1], padded_cond[:, 2:, 1:-1]),
        (padded_temp[:, 1:-1, :-2], padded_cond[:, 1:-1, :-2]),
        (padded_temp[:, 1:-1, 2:], padded_cond[:, 1:-1, 2:]),
    )
    for shift_temp, shift_cond in neighbours:
        net_flux = net_flux + 0.5 * (centre_cond + shift_cond) * (shift_temp - centre_temp)
    if centre_temp.shape[0] > 1:
        vertical = 0.5 * (centre_cond[1:] + centre_cond[:-1]) * (centre_temp[1:] - centre_temp[:-1])
        net_flux = (
            net_flux
            + jnp.pad(vertical, ((0, 1), (0, 0), (0, 0)))
            - jnp.pad(vertical, ((1, 0), (0, 0), (0, 0)))
        )
    return centre_temp + STEP_RATE * net_flux


def steps_kernel(
    depth_len, cond_ref, temp_ref, phase_ref, above_t, above_c, below_t, below_c,
    before_t, before_c, after_t, after_c, out_ref, temps, conds, nexts,
):
    step = pl.program_id(0)
    rows, cols = out_ref.shape[1], out_ref.shape[2]
    chunks = rows // ROWS
    wide = cols + 2 * LANES

    def conductance_step(plane, source, slots, chunk):
        cond_slots = conds.shape[0]
        upper = jnp.maximum(plane - 1, 0)
        lower = jnp.minimum(plane + 1, depth_len - 1)

        def get(ref, index, which):
            start = pl.multiple_of(which * ROWS, ROWS)
            return ref[index, pl.ds(start, ROWS), :]

        row = lax.broadcasted_iota(jnp.int32, (ROWS, wide), 0)
        prev = jnp.maximum(chunk - 1, 0)
        after = jnp.minimum(chunk + 1, chunks + 1)

        def around(ref, index):
            here = get(ref, index, chunk)
            up = jnp.where(
                row == 0, pltpu.roll(get(ref, index, prev), 1, 0), pltpu.roll(here, 1, 0)
            )
            down = jnp.where(
                row == ROWS - 1,
                pltpu.roll(get(ref, index, after), ROWS - 1, 0),
                pltpu.roll(here, ROWS - 1, 0),
            )
            return here, up, down

        temp, temp_up, temp_down = around(source, plane % slots)
        cond, cond_up, cond_down = around(conds, plane % cond_slots)
        east = (cond + pltpu.roll(cond, wide - 1, 1)) * (pltpu.roll(temp, wide - 1, 1) - temp)
        net = east - pltpu.roll(east, 1, 1)
        net += (cond + cond_up) * (temp_up - temp) + (cond + cond_down) * (temp_down - temp)
        for other in (upper, lower):
            other_cond = get(conds, other % cond_slots, chunk)
            net += (cond + other_cond) * (get(source, other % slots, chunk) - temp)
        return temp + (0.5 * STEP_RATE) * net

    @pl.when(step < depth_len)
    def _():
        def place(ref, slot, centre, above, below, before, after):
            ref[slot, ROWS : ROWS + rows, LANES : LANES + cols] = centre
            ref[slot, :ROWS, LANES : LANES + cols] = above[0]
            ref[slot, ROWS + rows :, LANES : LANES + cols] = below[0]
            ref[slot, :, :LANES] = before[0]
            ref[slot, :, LANES + cols :] = after[0]

        phases = jnp.where(phase_ref[0] == 1, cond_ref[1], cond_ref[0])
        place(temps, step % 3, temp_ref[0], above_t, below_t, before_t, after_t)
        place(conds, step % 4, phases, above_c, below_c, before_c, after_c)

    @pl.when((step >= 1) & (step <= depth_len))
    def _():
        @pl.loop(0, chunks + 2)
        def _(chunk):
            start = pl.multiple_of(chunk * ROWS, ROWS)
            nexts[(step - 1) % 3, pl.ds(start, ROWS), :] = conductance_step(
                step - 1, temps, 3, chunk
            )

    @pl.when(step >= 2)
    def _():
        @pl.loop(0, chunks)
        def _(chunk):
            start = pl.multiple_of(chunk * ROWS, ROWS)
            result = conductance_step(step - 2, nexts, 3, chunk + 1)
            out_ref[0, pl.ds(start, ROWS), :] = result[:, LANES : LANES + cols]


def two_steps(solid_temp, phase_map, phase_conductivity, above, below, before, after):
    depth_len, rows, cols = solid_temp.shape
    tall, wide = rows + 2 * ROWS, cols + 2 * LANES
    before = jnp.pad(before, ((0, 0), (0, 0), (LANES - WIDTH, 0)))
    after = jnp.pad(after, ((0, 0), (0, 0), (0, LANES - WIDTH)))

    def spec(*shape, offset=0):
        return pl.BlockSpec(
            (1,) + shape, lambda i: (jnp.minimum(i, depth_len - 1) + offset, 0, 0)
        )

    def pair(*shape):
        return [spec(*shape), spec(*shape, offset=depth_len)]

    return pl.pallas_call(
        functools.partial(steps_kernel, depth_len),
        grid=(depth_len + 2,),
        in_specs=[
            pl.BlockSpec(memory_space=pltpu.SMEM),
            spec(rows, cols),
            spec(rows, cols),
            *pair(ROWS, cols),
            *pair(ROWS, cols),
            *pair(tall, LANES),
            *pair(tall, LANES),
        ],
        out_specs=pl.BlockSpec((1, rows, cols), lambda i: (jnp.maximum(i - 2, 0), 0, 0)),
        out_shape=jax.ShapeDtypeStruct((depth_len, rows, cols), jnp.float32),
        scratch_shapes=[
            pltpu.VMEM((3, tall, wide), jnp.float32),
            pltpu.VMEM((4, tall, wide), jnp.float32),
            pltpu.VMEM((3, tall, wide), jnp.float32),
        ],
        compiler_params=params(),
        cost_estimate=pl.CostEstimate(
            flops=60 * depth_len * rows * cols,
            bytes_accessed=16 * depth_len * rows * cols,
            transcendentals=0,
        ),
        name="conduct_twice",
    )(
        phase_conductivity, solid_temp, phase_map,
        above, above, below, below, before, before, after, after,
    )


def per_device(pressure_source, solid_temp, gas_wall_temp, phase_map, phase_conductivity):
    groups = lax.axis_size("grp")
    pencils = lax.axis_size("pen")
    group_idx = lax.axis_index("grp")
    pencil_idx = lax.axis_index("pen")
    depth_loc, span_len, stream_loc = pressure_source.shape
    stream_len = stream_loc * pencils
    depth_len = depth_loc * groups
    half = span_len // 2
    waves_loc = span_len // groups
    steps = stream_loc // SEGMENTS
    f32 = jnp.float32

    order = wave_order(span_len, groups)
    row = np.arange(half)
    table = np.stack([cas(row[:, None] * (2 * row + parity)[None, :], span_len) for parity in (0, 1)])
    table_high = table.astype(jnp.bfloat16)
    table_low = (table - table_high.astype(np.float64)).astype(jnp.bfloat16)
    table_parts = jnp.asarray(np.stack([table_high, table_low], axis=1))
    lambdas, vectors = depth_modes(depth_len)
    eigen_span = 2.0 * np.cos(2.0 * math.pi * order / span_len) - 2.0
    shift = lambdas[None, :, None] - eigen_span[:, None, :]
    root = 2.0 / (shift + 2.0 + np.sqrt(shift * (shift + 4.0)))
    gain = -1.0 / (1.0 / root - root) / span_len
    around = np.arange(pencils)[:, None, None, None]
    reach = np.power(root, stream_loc * around) / (1.0 - np.power(root, stream_len))

    def mine(constant, axis):
        chosen = lax.dynamic_index_in_dim(jnp.asarray(constant, f32), group_idx, axis, keepdims=False)
        return chosen

    root_loc = mine(root, 0)
    gain_loc = mine(gain, 0)
    hop_loc = mine(np.power(root, steps), 0)
    reach_loc = mine(reach, 1)
    falling = jnp.roll(jnp.flip(reach_loc, 0), 1, 0)
    reach_left = lax.dynamic_slice_in_dim(
        jnp.concatenate([falling, falling]), (pencils + 1 - pencil_idx) % pencils, pencils, 0
    )
    reach_right = lax.dynamic_slice_in_dim(
        jnp.concatenate([reach_loc, reach_loc]), (2 * pencils - 1 - pencil_idx) % pencils, pencils, 0
    )

    tile_rows = span_len // groups

    def conductivity(phases):
        return jnp.where(phases == 1, phase_conductivity[1], phase_conductivity[0])

    solid_len = solid_temp.shape[0]
    edge_rows = [
        jnp.concatenate([solid_temp[:, part], conductivity(phase_map[:, part]), gas_wall_temp[None, part]])
        for part in (slice(0, ROWS), slice(tile_rows - ROWS, tile_rows))
    ]
    above, below = swap_edges(jnp.concatenate(edge_rows, axis=1), "grp", 1, ROWS)
    edge_cols = []
    for part in (slice(0, WIDTH), slice(stream_loc - WIDTH, stream_loc)):
        inner = jnp.concatenate(
            [solid_temp[:, :, part], conductivity(phase_map[:, :, part]), gas_wall_temp[None, :, part]]
        )
        edge_cols.append(jnp.concatenate([above[:, :, part], inner, below[:, :, part]], axis=1))
    before, after = swap_edges(jnp.concatenate(edge_cols, axis=2), "pen", 2, WIDTH)

    spectral = pl.pallas_call(
        span_forward_kernel,
        grid=(depth_loc,),
        in_specs=[
            pl.BlockSpec((1, span_len, stream_loc), lambda z: (z, 0, 0)),
            pl.BlockSpec((2, 2, half, half), lambda z: (0, 0, 0, 0)),
        ],
        out_specs=pl.BlockSpec((groups, 1, stream_loc, waves_loc), lambda z: (0, z, 0, 0)),
        out_shape=jax.ShapeDtypeStruct((groups, depth_loc, stream_loc, waves_loc), f32),
        compiler_params=params(),
        cost_estimate=pl.CostEstimate(
            flops=6 * depth_loc * stream_loc * span_len * half,
            bytes_accessed=8 * depth_loc * stream_loc * span_len,
            transcendentals=0,
        ),
        name="span_forward",
    )(pressure_source, table_parts)
    spectral, above, below, before, after = lax.optimization_barrier(
        (spectral, above, below, before, after)
    )
    unheated = two_steps(
        solid_temp, phase_map, phase_conductivity, above, below, before, after
    )

    def top_plane(inner, plane):
        rows = jnp.concatenate([above[plane, -1:], inner, below[plane, :1]])
        span = slice(ROWS - 1, ROWS + tile_rows + 1)
        return jnp.concatenate([before[plane, span, -1:], rows, after[plane, span, :1]], axis=1)

    top_cond = top_plane(conductivity(phase_map[0]), solid_len)
    dry_flux = top_plane(gas_wall_temp, 2 * solid_len) - top_plane(solid_temp[0], 0)
    moved = lax.all_to_all(spectral, "grp", split_axis=0, concat_axis=0, tiled=True)
    moved = moved.reshape(depth_len, stream_loc, waves_loc)

    data_spec = pl.BlockSpec((depth_len, stream_loc, LANES), lambda w: (0, 0, w))
    mode_spec = pl.BlockSpec((depth_len, steps, SEGMENTS, LANES), lambda w: (0, 0, 0, w))
    wave_spec = pl.BlockSpec((depth_len, 1, LANES), lambda w: (0, 0, w))
    ends_spec = pl.BlockSpec((depth_len, SEGMENTS, LANES), lambda w: (0, 0, w))
    ends_shape = jax.ShapeDtypeStruct((depth_len, SEGMENTS, waves_loc), f32)
    cost = pl.CostEstimate(
        flops=2 * depth_len**2 * stream_loc * waves_loc,
        bytes_accessed=8 * depth_len * stream_loc * waves_loc,
        transcendentals=0,
    )

    def rowed(value):
        return value[:, None, :]

    modes, heads, tails = pl.pallas_call(
        lambda s, r, m, h, t: ends_kernel(vectors, s, FirstRow(r), m, h, t),
        grid=(waves_loc // LANES,),
        in_specs=[data_spec, wave_spec],
        out_specs=[mode_spec, ends_spec, ends_spec],
        out_shape=[
            jax.ShapeDtypeStruct((depth_len, steps, SEGMENTS, waves_loc), f32),
            ends_shape,
            ends_shape,
        ],
        compiler_params=params(),
        cost_estimate=cost,
        name="stream_ends",
    )(moved, rowed(root_loc))
    tail_all = tails[:, 0]
    head_all = heads[:, SEGMENTS - 1]
    for part in range(1, SEGMENTS):
        tail_all = tails[:, part] + hop_loc * tail_all
        head_all = heads[:, SEGMENTS - 1 - part] + hop_loc * head_all
    gathered = lax.all_gather(jnp.stack([tail_all, head_all]), "pen")
    left = [jnp.sum(reach_left * gathered[:, 0], axis=0)]
    right = [jnp.sum(reach_right * gathered[:, 1], axis=0)]
    for part in range(SEGMENTS - 1):
        left.append(tails[:, part] + hop_loc * left[-1])
        right.append(heads[:, SEGMENTS - 1 - part] + hop_loc * right[-1])
    solved = pl.pallas_call(
        lambda m, r, g, a, b, o, c: solve_kernel(vectors, m, FirstRow(r), FirstRow(g), a, b, o, c),
        grid=(waves_loc // LANES,),
        in_specs=[mode_spec, wave_spec, wave_spec, ends_spec, ends_spec],
        out_specs=data_spec,
        out_shape=jax.ShapeDtypeStruct((depth_len, stream_loc, waves_loc), f32),
        scratch_shapes=[pltpu.VMEM((depth_len, steps, SEGMENTS, LANES), f32)],
        compiler_params=params(),
        cost_estimate=cost,
        name="stream_solve",
    )(modes, rowed(root_loc), rowed(gain_loc), jnp.stack(left, 1), jnp.stack(right[::-1], 1))

    returned = lax.all_to_all(
        solved.reshape(groups, depth_loc, stream_loc, waves_loc),
        "grp",
        split_axis=0,
        concat_axis=0,
        tiled=True,
    )
    pressure = pl.pallas_call(
        span_inverse_kernel,
        grid=(depth_loc,),
        in_specs=[
            pl.BlockSpec((groups, 1, stream_loc, waves_loc), lambda z: (0, z, 0, 0)),
            pl.BlockSpec((2, 2, half, half), lambda z: (0, 0, 0, 0)),
        ],
        out_specs=pl.BlockSpec((1, span_len, stream_loc), lambda z: (z, 0, 0)),
        out_shape=jax.ShapeDtypeStruct((depth_loc, span_len, stream_loc), f32),
        compiler_params=params(),
        cost_estimate=pl.CostEstimate(
            flops=6 * depth_loc * stream_loc * span_len * half,
            bytes_accessed=8 * depth_loc * stream_loc * span_len,
            transcendentals=0,
        ),
        name="span_inverse",
    )(returned, table_parts)

    span_rows = np.arange(-1, span_len + 1) % span_len
    wall_table = cas(span_rows[:, None] * order.reshape(1, -1), span_len)
    wall_rows = lax.dynamic_slice_in_dim(
        jnp.asarray(wall_table, f32), group_idx * tile_rows, tile_rows + 2, 0
    )
    wall_waves = lax.all_gather(solved[0], "grp")
    wall = jnp.einsum(
        "ygk,gxk->yx",
        wall_rows.reshape(tile_rows + 2, groups, waves_loc),
        wall_waves,
        precision=HIGH,
        preferred_element_type=f32,
    )
    wall_left, wall_right = swap_edges(wall, "pen", 1, 1)
    wall = jnp.concatenate([wall_left, wall, wall_right], axis=1)
    flux = (HEAT_TRANSFER * (dry_flux + PRESSURE_WORK * wall))[None]
    centre_flux = flux[0, 1:-1, 1:-1]
    between = 0.5 * (top_cond[1:-1, 1:-1] + conductivity(phase_map[1])) * centre_flux
    lateral = conduct(flux, top_cond[None])[0]
    top = STEP_RATE * (centre_flux + lateral - STEP_RATE * between)
    second = STEP_RATE * STEP_RATE * between
    final_temp = unheated.at[0].add(top).at[1].add(second)
    return (pressure, final_temp)


class FirstRow:
    def __init__(self, ref):
        self.ref = ref

    def __getitem__(self, mode):
        return self.ref[mode, 0]


def solution(mesh):
    in_specs = (
        P("grp", None, "pen"),
        P(None, "grp", "pen"),
        P("grp", "pen"),
        P(None, "grp", "pen"),
        P(),
    )
    out_specs = (P("grp", None, "pen"), P(None, "grp", "pen"))
    return jax.shard_map(
        per_device, mesh=mesh, in_specs=in_specs, out_specs=out_specs, check_vma=False
    )
```

```python
import functools
import math

import jax
import jax.numpy as jnp
import numpy as np
from jax import lax
from jax.experimental import pallas as pl
from jax.experimental.pallas import tpu as pltpu
from jax.sharding import PartitionSpec as P

HIGH = lax.Precision.HIGH
HEAT_TRANSFER = 1.0
PRESSURE_WORK = 0.5
STEP_RATE = 0.12
LANES = 128
SEGMENTS = 8
ROWS = 8
WIDTH = 2
VMEM_BYTES = 56 * 2**20


def params():
    return pltpu.CompilerParams(vmem_limit_bytes=VMEM_BYTES)


def swap_edges(cells, axis, dim, width):
    count = lax.axis_size(axis)
    head = lax.slice_in_dim(cells, 0, width, axis=dim)
    tail = lax.slice_in_dim(cells, cells.shape[dim] - width, cells.shape[dim], axis=dim)
    return (
        lax.ppermute(tail, axis, [(i, (i + 1) % count) for i in range(count)]),
        lax.ppermute(head, axis, [((i + 1) % count, i) for i in range(count)]),
    )


def cas(product, length):
    angle = (product % length) * (2.0 * math.pi / length)
    return np.cos(angle) + np.sin(angle)


def depth_modes(depth_len):
    matrix = np.diag(np.full(depth_len, -2.0))
    matrix += np.diag(np.ones(depth_len - 1), 1) + np.diag(np.ones(depth_len - 1), -1)
    matrix[0, 0] = -1.0
    values, vectors = np.linalg.eigh(matrix)
    return -values, vectors.T


def wave_order(span_len, groups):
    order = np.concatenate([np.arange(0, span_len, 2), np.arange(1, span_len, 2)])
    return order.reshape(groups, span_len // groups)


def split(value):
    high = value.astype(jnp.bfloat16)
    low = (value - high.astype(jnp.float32)).astype(jnp.bfloat16)
    return high, low


def dot_split(left, right, dims):
    dot = functools.partial(
        lax.dot_general, dimension_numbers=(dims, ((), ())), preferred_element_type=jnp.float32
    )
    return dot(left[0], right[0]) + dot(left[0], right[1]) + dot(left[1], right[0])


def span_forward_kernel(source_ref, table_ref, out_ref):
    half = table_ref.shape[2]
    lots, width = out_ref.shape[0], out_ref.shape[4]
    head = source_ref[0, :half]
    tail = source_ref[0, half:]
    for parity in range(2):
        folded = split(head - tail if parity else head + tail)
        table = (table_ref[parity, 0], table_ref[parity, 1])
        result = dot_split(folded, table, ((0,), (0,)))
        per = half // width
        for part in range(per):
            group = parity * (per // lots) + part // lots
            out_ref[part % lots, group, 0] = result[:, part * width : (part + 1) * width]


def span_inverse_kernel(*refs):
    waves_refs, table_ref, out_ref = refs[:-2], refs[-2], refs[-1]
    half = table_ref.shape[2]
    per = waves_refs[0].shape[0] // 2
    halves = []
    for parity in range(2):
        table = (table_ref[parity, 0], table_ref[parity, 1])
        waves = jnp.concatenate(
            [ref[parity * per + part, 0] for part in range(per) for ref in waves_refs], axis=1
        )
        halves.append(dot_split(table, split(waves), ((1,), (1,))))
    out_ref[0, :half] = halves[0] + halves[1]
    out_ref[0, half:] = halves[0] - halves[1]


def mix(weights, planes):
    result = []
    for row in weights:
        total = float(row[0]) * planes[0]
        for weight, plane in zip(row[1:], planes[1:]):
            total = total + float(weight) * plane
        result.append(total)
    return result


def ends_kernel(vectors, source_ref, root_ref, modes_ref, head_ref, tail_ref):
    depth_len, steps = modes_ref.shape[0], modes_ref.shape[1]

    def ahead(step, carry):
        planes = [
            source_ref[plane, pl.ds(step, SEGMENTS, stride=steps), :] for plane in range(depth_len)
        ]
        made = []
        for mode, value in enumerate(mix(vectors, planes)):
            modes_ref[mode, step] = value
            made.append(value + root_ref[mode][None] * carry[mode])
        return tuple(made)

    def back(step, carry):
        return tuple(
            modes_ref[mode, steps - 1 - step] + root_ref[mode][None] * carry[mode]
            for mode in range(depth_len)
        )

    zero = tuple(jnp.zeros((SEGMENTS, LANES), jnp.float32) for _ in range(depth_len))
    ended = lax.fori_loop(0, steps, ahead, zero)
    for mode in range(depth_len):
        tail_ref[mode] = ended[mode]
    ended = lax.fori_loop(0, steps, back, zero)
    for mode in range(depth_len):
        head_ref[mode] = ended[mode]


def solve_kernel(vectors, modes_ref, root_ref, gain_ref, left_ref, right_ref, out_ref, ahead_ref):
    depth_len, steps = modes_ref.shape[0], modes_ref.shape[1]

    def ahead(step, carry):
        made = []
        for mode in range(depth_len):
            value = modes_ref[mode, step] + root_ref[mode][None] * carry[mode]
            ahead_ref[mode, step] = value
            made.append(value)
        return tuple(made)

    def back(count, carry):
        step = steps - 1 - count
        made, solved = [], []
        for mode in range(depth_len):
            coming = root_ref[mode][None] * carry[mode]
            solved.append(gain_ref[mode][None] * (ahead_ref[mode, step] + coming))
            made.append(modes_ref[mode, step] + coming)
        for plane, value in enumerate(mix(vectors.T, solved)):
            out_ref[plane, pl.ds(step, SEGMENTS, stride=steps), :] = value
        return tuple(made)

    lax.fori_loop(0, steps, ahead, tuple(left_ref[mode] for mode in range(depth_len)))
    lax.fori_loop(0, steps, back, tuple(right_ref[mode] for mode in range(depth_len)))


def conduct(padded_temp, padded_cond):
    centre_temp = padded_temp[:, 1:-1, 1:-1]
    centre_cond = padded_cond[:, 1:-1, 1:-1]
    net_flux = jnp.zeros_like(centre_temp)
    neighbours = (
        (padded_temp[:, :-2, 1:-1], padded_cond[:, :-2, 1:-1]),
        (padded_temp[:, 2:, 1:-1], padded_cond[:, 2:, 1:-1]),
        (padded_temp[:, 1:-1, :-2], padded_cond[:, 1:-1, :-2]),
        (padded_temp[:, 1:-1, 2:], padded_cond[:, 1:-1, 2:]),
    )
    for shift_temp, shift_cond in neighbours:
        net_flux = net_flux + 0.5 * (centre_cond + shift_cond) * (shift_temp - centre_temp)
    if centre_temp.shape[0] > 1:
        vertical = 0.5 * (centre_cond[1:] + centre_cond[:-1]) * (centre_temp[1:] - centre_temp[:-1])
        net_flux = (
            net_flux
            + jnp.pad(vertical, ((0, 1), (0, 0), (0, 0)))
            - jnp.pad(vertical, ((1, 0), (0, 0), (0, 0)))
        )
    return centre_temp + STEP_RATE * net_flux


def steps_kernel(
    depth_len, cond_ref, temp_ref, phase_ref, above_t, above_c, below_t, below_c,
    side_t, side_c, out_ref, temps, conds, nexts,
):
    step = pl.program_id(0)
    rows, cols = out_ref.shape[1], out_ref.shape[2]
    chunks = rows // ROWS
    wide = cols + LANES

    def conductance_step(plane, source, slots, chunk):
        cond_slots = conds.shape[0]
        upper = jnp.maximum(plane - 1, 0)
        lower = jnp.minimum(plane + 1, depth_len - 1)

        start = pl.multiple_of(chunk * ROWS, ROWS)
        tall = 2 * ROWS

        def get(ref, index):
            return ref[index, pl.ds(start + ROWS, tall), :]

        def around(ref, index):
            window = ref[index, pl.ds(start, tall + 2 * ROWS), :]
            return (
                window[ROWS : ROWS + tall],
                window[ROWS - 1 : ROWS - 1 + tall],
                window[ROWS + 1 : ROWS + 1 + tall],
            )

        temp, temp_up, temp_down = around(source, plane % slots)
        cond, cond_up, cond_down = around(conds, plane % cond_slots)
        east = (cond + pltpu.roll(cond, wide - 1, 1)) * (pltpu.roll(temp, wide - 1, 1) - temp)
        net = east - pltpu.roll(east, 1, 1)
        net += (cond + cond_up) * (temp_up - temp) + (cond + cond_down) * (temp_down - temp)
        for other in (upper, lower):
            other_cond = get(conds, other % cond_slots)
            net += (cond + other_cond) * (get(source, other % slots) - temp)
        return temp + (0.5 * STEP_RATE) * net

    @pl.when(step < depth_len)
    def _():
        def place(ref, slot, centre, above, below, side):
            ref[slot, 2 * ROWS : 2 * ROWS + rows, :cols] = centre
            ref[slot, ROWS : 2 * ROWS, :cols] = above[0]
            ref[slot, 2 * ROWS + rows : 3 * ROWS + rows, :cols] = below[0]
            ref[slot, ROWS : 3 * ROWS + rows, cols:] = side[0]

        phases = jnp.where(phase_ref[0] == 1, cond_ref[1], cond_ref[0])
        place(temps, step % 3, temp_ref[0], above_t, below_t, side_t)
        place(conds, step % 4, phases, above_c, below_c, side_c)

    @pl.when((step >= 1) & (step <= depth_len))
    def _():
        @pl.loop(0, (chunks + 2) // 2)
        def _(pair):
            start = pl.multiple_of(2 * pair * ROWS, ROWS) + ROWS
            nexts[(step - 1) % 3, pl.ds(start, 2 * ROWS), :] = conductance_step(
                step - 1, temps, 3, 2 * pair
            )

    @pl.when(step >= 2)
    def _():
        @pl.loop(0, chunks // 2)
        def _(pair):
            start = pl.multiple_of(2 * pair * ROWS, ROWS)
            result = conductance_step(step - 2, nexts, 3, 2 * pair + 1)
            out_ref[0, pl.ds(start, 2 * ROWS), :] = result[:, :cols]


def two_steps(solid_temp, phase_map, phase_conductivity, above, below, before, after):
    depth_len, rows, cols = solid_temp.shape
    tall, wide = rows + 2 * ROWS, cols + LANES
    gap = jnp.zeros(before.shape[:2] + (LANES - 2 * WIDTH,), jnp.float32)
    side = jnp.concatenate([after, gap, before], axis=2)

    def spec(*shape, offset=0):
        return pl.BlockSpec(
            (1,) + shape, lambda i: (jnp.minimum(i, depth_len - 1) + offset, 0, 0)
        )

    def pair(*shape):
        return [spec(*shape), spec(*shape, offset=depth_len)]

    return pl.pallas_call(
        functools.partial(steps_kernel, depth_len),
        grid=(depth_len + 2,),
        in_specs=[
            pl.BlockSpec(memory_space=pltpu.SMEM),
            spec(rows, cols),
            spec(rows, cols),
            *pair(ROWS, cols),
            *pair(ROWS, cols),
            *pair(tall, LANES),
        ],
        out_specs=pl.BlockSpec((1, rows, cols), lambda i: (jnp.maximum(i - 2, 0), 0, 0)),
        out_shape=jax.ShapeDtypeStruct((depth_len, rows, cols), jnp.float32),
        scratch_shapes=[
            pltpu.VMEM((3, tall + 2 * ROWS, wide), jnp.float32),
            pltpu.VMEM((4, tall + 2 * ROWS, wide), jnp.float32),
            pltpu.VMEM((3, tall + 2 * ROWS, wide), jnp.float32),
        ],
        compiler_params=params(),
        cost_estimate=pl.CostEstimate(
            flops=60 * depth_len * rows * cols,
            bytes_accessed=16 * depth_len * rows * cols,
            transcendentals=0,
        ),
        name="conduct_twice",
    )(
        phase_conductivity, solid_temp, phase_map,
        above, above, below, below, side, side,
    )


def per_device(pressure_source, solid_temp, gas_wall_temp, phase_map, phase_conductivity):
    groups = lax.axis_size("grp")
    pencils = lax.axis_size("pen")
    group_idx = lax.axis_index("grp")
    pencil_idx = lax.axis_index("pen")
    depth_loc, span_len, stream_loc = pressure_source.shape
    stream_len = stream_loc * pencils
    depth_len = depth_loc * groups
    half = span_len // 2
    waves_loc = span_len // groups
    steps = stream_loc // SEGMENTS
    f32 = jnp.float32

    lots = waves_loc // LANES

    order = wave_order(span_len, groups)
    row = np.arange(half)
    table = np.stack([cas(row[:, None] * (2 * row + parity)[None, :], span_len) for parity in (0, 1)])
    table_high = table.astype(jnp.bfloat16)
    table_low = (table - table_high.astype(np.float64)).astype(jnp.bfloat16)
    table_parts = jnp.asarray(np.stack([table_high, table_low], axis=1))
    lambdas, vectors = depth_modes(depth_len)
    eigen_span = 2.0 * np.cos(2.0 * math.pi * order / span_len) - 2.0
    shift = lambdas[None, :, None] - eigen_span[:, None, :]
    root = 2.0 / (shift + 2.0 + np.sqrt(shift * (shift + 4.0)))
    gain = -1.0 / (1.0 / root - root) / span_len
    around = np.arange(pencils)[:, None, None, None]
    reach = np.power(root, stream_loc * around) / (1.0 - np.power(root, stream_len))

    def mine(constant, axis):
        chosen = lax.dynamic_index_in_dim(jnp.asarray(constant, f32), group_idx, axis, keepdims=False)
        return chosen

    root_loc = mine(root, 0)
    gain_loc = mine(gain, 0)
    hop_loc = mine(np.power(root, steps), 0)
    reach_loc = mine(reach, 1)
    falling = jnp.roll(jnp.flip(reach_loc, 0), 1, 0)
    reach_left = lax.dynamic_slice_in_dim(
        jnp.concatenate([falling, falling]), (pencils + 1 - pencil_idx) % pencils, pencils, 0
    )
    reach_right = lax.dynamic_slice_in_dim(
        jnp.concatenate([reach_loc, reach_loc]), (2 * pencils - 1 - pencil_idx) % pencils, pencils, 0
    )

    tile_rows = span_len // groups

    def conductivity(phases):
        return jnp.where(phases == 1, phase_conductivity[1], phase_conductivity[0])

    solid_len = solid_temp.shape[0]
    edge_rows = [
        jnp.concatenate([solid_temp[:, part], conductivity(phase_map[:, part]), gas_wall_temp[None, part]])
        for part in (slice(0, ROWS), slice(tile_rows - ROWS, tile_rows))
    ]
    above, below = swap_edges(jnp.concatenate(edge_rows, axis=1), "grp", 1, ROWS)
    edge_cols = []
    for part in (slice(0, WIDTH), slice(stream_loc - WIDTH, stream_loc)):
        inner = jnp.concatenate(
            [solid_temp[:, :, part], conductivity(phase_map[:, :, part]), gas_wall_temp[None, :, part]]
        )
        edge_cols.append(jnp.concatenate([above[:, :, part], inner, below[:, :, part]], axis=1))
    before, after = swap_edges(jnp.concatenate(edge_cols, axis=2), "pen", 2, WIDTH)

    spectral = pl.pallas_call(
        span_forward_kernel,
        grid=(depth_loc,),
        in_specs=[
            pl.BlockSpec((1, span_len, stream_loc), lambda z: (z, 0, 0)),
            pl.BlockSpec((2, 2, half, half), lambda z: (0, 0, 0, 0)),
        ],
        out_specs=pl.BlockSpec((lots, groups, 1, stream_loc, LANES), lambda z: (0, 0, z, 0, 0)),
        out_shape=jax.ShapeDtypeStruct((lots, groups, depth_loc, stream_loc, LANES), f32),
        compiler_params=params(),
        cost_estimate=pl.CostEstimate(
            flops=6 * depth_loc * stream_loc * span_len * half,
            bytes_accessed=8 * depth_loc * stream_loc * span_len,
            transcendentals=0,
        ),
        name="span_forward",
    )(pressure_source, table_parts)
    unheated = two_steps(
        solid_temp, phase_map, phase_conductivity, above, below, before, after
    )

    def top_plane(inner, plane):
        rows = jnp.concatenate([above[plane, -1:], inner, below[plane, :1]])
        span = slice(ROWS - 1, ROWS + tile_rows + 1)
        return jnp.concatenate([before[plane, span, -1:], rows, after[plane, span, :1]], axis=1)

    top_cond = top_plane(conductivity(phase_map[0]), solid_len)
    dry_flux = top_plane(gas_wall_temp, 2 * solid_len) - top_plane(solid_temp[0], 0)
    data_spec = pl.BlockSpec((depth_len, stream_loc, LANES), lambda w: (0, 0, w))
    mode_spec = pl.BlockSpec((depth_len, steps, SEGMENTS, LANES), lambda w: (0, 0, 0, w))
    wave_spec = pl.BlockSpec((depth_len, 1, LANES), lambda w: (0, 0, w))
    ends_spec = pl.BlockSpec((depth_len, SEGMENTS, LANES), lambda w: (0, 0, w))
    ends_shape = jax.ShapeDtypeStruct((depth_len, SEGMENTS, LANES), f32)
    cost = pl.CostEstimate(
        flops=2 * depth_len**2 * stream_loc * waves_loc,
        bytes_accessed=8 * depth_len * stream_loc * waves_loc,
        transcendentals=0,
    )

    def rowed(value):
        return value[:, None, :]

    def lot_of(value, lot):
        return value[..., lot * LANES : (lot + 1) * LANES]

    solved_top, returned = [], []
    for lot in range(lots):
        roots, gains, hops = (lot_of(value, lot) for value in (root_loc, gain_loc, hop_loc))
        lefts, rights = lot_of(reach_left, lot), lot_of(reach_right, lot)
        moved = lax.all_to_all(spectral[lot], "grp", split_axis=0, concat_axis=0, tiled=True)
        moved = moved.reshape(depth_len, stream_loc, LANES)
        modes, heads, tails = pl.pallas_call(
            lambda s, r, m, h, t: ends_kernel(vectors, s, FirstRow(r), m, h, t),
            grid=(1,),
            in_specs=[data_spec, wave_spec],
            out_specs=[mode_spec, ends_spec, ends_spec],
            out_shape=[
                jax.ShapeDtypeStruct((depth_len, steps, SEGMENTS, LANES), f32),
                ends_shape,
                ends_shape,
            ],
            compiler_params=params(),
            cost_estimate=cost,
            name="stream_ends",
        )(moved, rowed(roots))
        tail_all = tails[:, 0]
        head_all = heads[:, SEGMENTS - 1]
        for part in range(1, SEGMENTS):
            tail_all = tails[:, part] + hops * tail_all
            head_all = heads[:, SEGMENTS - 1 - part] + hops * head_all
        gathered = lax.all_gather(jnp.stack([tail_all, head_all]), "pen")
        left = [jnp.sum(lefts * gathered[:, 0], axis=0)]
        right = [jnp.sum(rights * gathered[:, 1], axis=0)]
        for part in range(SEGMENTS - 1):
            left.append(tails[:, part] + hops * left[-1])
            right.append(heads[:, SEGMENTS - 1 - part] + hops * right[-1])
        solved = pl.pallas_call(
            lambda m, r, g, a, b, o, c: solve_kernel(vectors, m, FirstRow(r), FirstRow(g), a, b, o, c),
            grid=(1,),
            in_specs=[mode_spec, wave_spec, wave_spec, ends_spec, ends_spec],
            out_specs=data_spec,
            out_shape=jax.ShapeDtypeStruct((depth_len, stream_loc, LANES), f32),
            scratch_shapes=[pltpu.VMEM((depth_len, steps, SEGMENTS, LANES), f32)],
            compiler_params=params(),
            cost_estimate=cost,
            name="stream_solve",
        )(modes, rowed(roots), rowed(gains), jnp.stack(left, 1), jnp.stack(right[::-1], 1))

        back = lax.all_to_all(
            solved.reshape(groups, depth_loc, stream_loc, LANES),
            "grp",
            split_axis=0,
            concat_axis=0,
            tiled=True,
        )
        solved_top.append(solved[0])
        returned.append(back)

    pressure = pl.pallas_call(
        span_inverse_kernel,
        grid=(depth_loc,),
        in_specs=[
            *[pl.BlockSpec((groups, 1, stream_loc, LANES), lambda z: (0, z, 0, 0))] * lots,
            pl.BlockSpec((2, 2, half, half), lambda z: (0, 0, 0, 0)),
        ],
        out_specs=pl.BlockSpec((1, span_len, stream_loc), lambda z: (z, 0, 0)),
        out_shape=jax.ShapeDtypeStruct((depth_loc, span_len, stream_loc), f32),
        compiler_params=params(),
        cost_estimate=pl.CostEstimate(
            flops=6 * depth_loc * stream_loc * span_len * half,
            bytes_accessed=8 * depth_loc * stream_loc * span_len,
            transcendentals=0,
        ),
        name="span_inverse",
    )(*returned, table_parts)

    span_rows = np.arange(-1, span_len + 1) % span_len
    wall_table = cas(span_rows[:, None] * order.reshape(1, -1), span_len)
    wall_rows = lax.dynamic_slice_in_dim(
        jnp.asarray(wall_table, f32), group_idx * tile_rows, tile_rows + 2, 0
    )
    wall_waves = lax.all_gather(jnp.concatenate(solved_top, axis=1), "grp")
    wall = jnp.einsum(
        "ygk,gxk->yx",
        wall_rows.reshape(tile_rows + 2, groups, waves_loc),
        wall_waves,
        precision=HIGH,
        preferred_element_type=f32,
    )
    wall_left, wall_right = swap_edges(wall, "pen", 1, 1)
    wall = jnp.concatenate([wall_left, wall, wall_right], axis=1)
    flux = (HEAT_TRANSFER * (dry_flux + PRESSURE_WORK * wall))[None]
    centre_flux = flux[0, 1:-1, 1:-1]
    between = 0.5 * (top_cond[1:-1, 1:-1] + conductivity(phase_map[1])) * centre_flux
    lateral = conduct(flux, top_cond[None])[0]
    top = STEP_RATE * (centre_flux + lateral - STEP_RATE * between)
    second = STEP_RATE * STEP_RATE * between
    final_temp = unheated.at[0].add(top).at[1].add(second)
    return (pressure, final_temp)


class FirstRow:
    def __init__(self, ref):
        self.ref = ref

    def __getitem__(self, mode):
        return self.ref[mode, 0]


def solution(mesh):
    in_specs = (
        P("grp", None, "pen"),
        P(None, "grp", "pen"),
        P("grp", "pen"),
        P(None, "grp", "pen"),
        P(),
    )
    out_specs = (P("grp", None, "pen"), P(None, "grp", "pen"))
    return jax.shard_map(
        per_device, mesh=mesh, in_specs=in_specs, out_specs=out_specs, check_vma=False
    )
```

```python
import functools
import math

import jax
import jax.numpy as jnp
import numpy as np
from jax import lax
from jax.experimental import pallas as pl
from jax.experimental.pallas import tpu as pltpu
from jax.sharding import PartitionSpec as P

HIGH = lax.Precision.HIGH
HEAT_TRANSFER = 1.0
PRESSURE_WORK = 0.5
STEP_RATE = 0.12
LANES = 128
SEGMENTS = 8
ROWS = 8
WIDTH = 2
VMEM_BYTES = 56 * 2**20


def params():
    return pltpu.CompilerParams(vmem_limit_bytes=VMEM_BYTES)


def swap_edges(cells, axis, dim, width):
    count = lax.axis_size(axis)
    head = lax.slice_in_dim(cells, 0, width, axis=dim)
    tail = lax.slice_in_dim(cells, cells.shape[dim] - width, cells.shape[dim], axis=dim)
    return (
        lax.ppermute(tail, axis, [(i, (i + 1) % count) for i in range(count)]),
        lax.ppermute(head, axis, [((i + 1) % count, i) for i in range(count)]),
    )


def cas(product, length):
    angle = (product % length) * (2.0 * math.pi / length)
    return np.cos(angle) + np.sin(angle)


def depth_modes(depth_len):
    matrix = np.diag(np.full(depth_len, -2.0))
    matrix += np.diag(np.ones(depth_len - 1), 1) + np.diag(np.ones(depth_len - 1), -1)
    matrix[0, 0] = -1.0
    values, vectors = np.linalg.eigh(matrix)
    return -values, vectors.T


def wave_order(span_len, groups):
    order = np.concatenate([np.arange(0, span_len, 2), np.arange(1, span_len, 2)])
    return order.reshape(groups, span_len // groups)


def split(value):
    high = value.astype(jnp.bfloat16)
    low = (value - high.astype(jnp.float32)).astype(jnp.bfloat16)
    return high, low


def dot_split(left, right, dims):
    dot = functools.partial(
        lax.dot_general, dimension_numbers=(dims, ((), ())), preferred_element_type=jnp.float32
    )
    return dot(left[0], right[0]) + dot(left[0], right[1]) + dot(left[1], right[0])


def span_forward_kernel(source_ref, table_ref, out_ref):
    half = table_ref.shape[2]
    width = out_ref.shape[3]
    head = source_ref[0, :half]
    tail = source_ref[0, half:]
    for parity in range(2):
        folded = split(head - tail if parity else head + tail)
        table = (table_ref[parity, 0], table_ref[parity, 1])
        result = dot_split(folded, table, ((0,), (0,)))
        per = half // width
        for part in range(per):
            out_ref[parity * per + part, 0] = result[:, part * width : (part + 1) * width]


def span_inverse_kernel(waves_ref, table_ref, out_ref):
    half = table_ref.shape[2]
    per = waves_ref.shape[0] // 2
    halves = []
    for parity in range(2):
        table = (table_ref[parity, 0], table_ref[parity, 1])
        waves = jnp.concatenate([waves_ref[parity * per + part, 0] for part in range(per)], axis=1)
        halves.append(dot_split(table, split(waves), ((1,), (1,))))
    out_ref[0, :half] = halves[0] + halves[1]
    out_ref[0, half:] = halves[0] - halves[1]


def mix(weights, planes):
    result = []
    for row in weights:
        total = float(row[0]) * planes[0]
        for weight, plane in zip(row[1:], planes[1:]):
            total = total + float(weight) * plane
        result.append(total)
    return result


def ends_kernel(vectors, source_ref, root_ref, modes_ref, head_ref, tail_ref):
    depth_len, steps = modes_ref.shape[0], modes_ref.shape[1]

    def ahead(step, carry):
        planes = [
            source_ref[plane, pl.ds(step, SEGMENTS, stride=steps), :] for plane in range(depth_len)
        ]
        made = []
        for mode, value in enumerate(mix(vectors, planes)):
            modes_ref[mode, step] = value
            made.append(value + root_ref[mode][None] * carry[mode])
        return tuple(made)

    def back(step, carry):
        return tuple(
            modes_ref[mode, steps - 1 - step] + root_ref[mode][None] * carry[mode]
            for mode in range(depth_len)
        )

    zero = tuple(jnp.zeros((SEGMENTS, LANES), jnp.float32) for _ in range(depth_len))
    ended = lax.fori_loop(0, steps, ahead, zero)
    for mode in range(depth_len):
        tail_ref[mode] = ended[mode]
    ended = lax.fori_loop(0, steps, back, zero)
    for mode in range(depth_len):
        head_ref[mode] = ended[mode]


def solve_kernel(vectors, modes_ref, root_ref, gain_ref, left_ref, right_ref, out_ref, ahead_ref):
    depth_len, steps = modes_ref.shape[0], modes_ref.shape[1]

    def ahead(step, carry):
        made = []
        for mode in range(depth_len):
            value = modes_ref[mode, step] + root_ref[mode][None] * carry[mode]
            ahead_ref[mode, step] = value
            made.append(value)
        return tuple(made)

    def back(count, carry):
        step = steps - 1 - count
        made, solved = [], []
        for mode in range(depth_len):
            coming = root_ref[mode][None] * carry[mode]
            solved.append(gain_ref[mode][None] * (ahead_ref[mode, step] + coming))
            made.append(modes_ref[mode, step] + coming)
        for plane, value in enumerate(mix(vectors.T, solved)):
            out_ref[plane, pl.ds(step, SEGMENTS, stride=steps), :] = value
        return tuple(made)

    lax.fori_loop(0, steps, ahead, tuple(left_ref[mode] for mode in range(depth_len)))
    lax.fori_loop(0, steps, back, tuple(right_ref[mode] for mode in range(depth_len)))


def conduct(padded_temp, padded_cond):
    centre_temp = padded_temp[:, 1:-1, 1:-1]
    centre_cond = padded_cond[:, 1:-1, 1:-1]
    net_flux = jnp.zeros_like(centre_temp)
    neighbours = (
        (padded_temp[:, :-2, 1:-1], padded_cond[:, :-2, 1:-1]),
        (padded_temp[:, 2:, 1:-1], padded_cond[:, 2:, 1:-1]),
        (padded_temp[:, 1:-1, :-2], padded_cond[:, 1:-1, :-2]),
        (padded_temp[:, 1:-1, 2:], padded_cond[:, 1:-1, 2:]),
    )
    for shift_temp, shift_cond in neighbours:
        net_flux = net_flux + 0.5 * (centre_cond + shift_cond) * (shift_temp - centre_temp)
    if centre_temp.shape[0] > 1:
        vertical = 0.5 * (centre_cond[1:] + centre_cond[:-1]) * (centre_temp[1:] - centre_temp[:-1])
        net_flux = (
            net_flux
            + jnp.pad(vertical, ((0, 1), (0, 0), (0, 0)))
            - jnp.pad(vertical, ((1, 0), (0, 0), (0, 0)))
        )
    return centre_temp + STEP_RATE * net_flux


def steps_kernel(
    depth_len, cond_ref, temp_ref, phase_ref, above_t, above_c, below_t, below_c,
    side_t, side_c, out_ref, temps, conds, nexts,
):
    step = pl.program_id(0)
    rows, cols = out_ref.shape[1], out_ref.shape[2]
    chunks = rows // ROWS
    wide = cols + LANES

    def conductance_step(plane, source, slots, chunk):
        cond_slots = conds.shape[0]
        upper = jnp.maximum(plane - 1, 0)
        lower = jnp.minimum(plane + 1, depth_len - 1)

        start = pl.multiple_of(chunk * ROWS, ROWS)
        tall = 2 * ROWS

        def get(ref, index):
            return ref[index, pl.ds(start + ROWS, tall), :]

        def around(ref, index):
            window = ref[index, pl.ds(start, tall + 2 * ROWS), :]
            return (
                window[ROWS : ROWS + tall],
                window[ROWS - 1 : ROWS - 1 + tall],
                window[ROWS + 1 : ROWS + 1 + tall],
            )

        temp, temp_up, temp_down = around(source, plane % slots)
        cond, cond_up, cond_down = around(conds, plane % cond_slots)
        east = (cond + pltpu.roll(cond, wide - 1, 1)) * (pltpu.roll(temp, wide - 1, 1) - temp)
        net = east - pltpu.roll(east, 1, 1)
        net += (cond + cond_up) * (temp_up - temp) + (cond + cond_down) * (temp_down - temp)
        for other in (upper, lower):
            other_cond = get(conds, other % cond_slots)
            net += (cond + other_cond) * (get(source, other % slots) - temp)
        return temp + (0.5 * STEP_RATE) * net

    @pl.when(step < depth_len)
    def _():
        def place(ref, slot, centre, above, below, side):
            ref[slot, 2 * ROWS : 2 * ROWS + rows, :cols] = centre
            ref[slot, ROWS : 2 * ROWS, :cols] = above[0]
            ref[slot, 2 * ROWS + rows : 3 * ROWS + rows, :cols] = below[0]
            ref[slot, ROWS : 3 * ROWS + rows, cols:] = side[0]

        phases = jnp.where(phase_ref[0] == 1, cond_ref[1], cond_ref[0])
        place(temps, step % 3, temp_ref[0], above_t, below_t, side_t)
        place(conds, step % 4, phases, above_c, below_c, side_c)

    @pl.when((step >= 1) & (step <= depth_len))
    def _():
        @pl.loop(0, (chunks + 2) // 2)
        def _(pair):
            start = pl.multiple_of(2 * pair * ROWS, ROWS) + ROWS
            nexts[(step - 1) % 3, pl.ds(start, 2 * ROWS), :] = conductance_step(
                step - 1, temps, 3, 2 * pair
            )

    @pl.when(step >= 2)
    def _():
        @pl.loop(0, chunks // 2)
        def _(pair):
            start = pl.multiple_of(2 * pair * ROWS, ROWS)
            result = conductance_step(step - 2, nexts, 3, 2 * pair + 1)
            out_ref[0, pl.ds(start, 2 * ROWS), :] = result[:, :cols]


def two_steps(solid_temp, phase_map, phase_conductivity, above, below, side):
    depth_len, rows, cols = solid_temp.shape
    tall, wide = rows + 2 * ROWS, cols + LANES
    def spec(*shape, offset=0):
        return pl.BlockSpec(
            (1,) + shape, lambda i: (jnp.minimum(i, depth_len - 1) + offset, 0, 0)
        )

    def pair(*shape):
        return [spec(*shape), spec(*shape, offset=depth_len)]

    return pl.pallas_call(
        functools.partial(steps_kernel, depth_len),
        grid=(depth_len + 2,),
        in_specs=[
            pl.BlockSpec(memory_space=pltpu.SMEM),
            spec(rows, cols),
            spec(rows, cols),
            *pair(ROWS, cols),
            *pair(ROWS, cols),
            *pair(tall, LANES),
        ],
        out_specs=pl.BlockSpec((1, rows, cols), lambda i: (jnp.maximum(i - 2, 0), 0, 0)),
        out_shape=jax.ShapeDtypeStruct((depth_len, rows, cols), jnp.float32),
        scratch_shapes=[
            pltpu.VMEM((3, tall + 2 * ROWS, wide), jnp.float32),
            pltpu.VMEM((4, tall + 2 * ROWS, wide), jnp.float32),
            pltpu.VMEM((3, tall + 2 * ROWS, wide), jnp.float32),
        ],
        compiler_params=params(),
        cost_estimate=pl.CostEstimate(
            flops=60 * depth_len * rows * cols,
            bytes_accessed=16 * depth_len * rows * cols,
            transcendentals=0,
        ),
        name="conduct_twice",
    )(
        phase_conductivity, solid_temp, phase_map,
        above, above, below, below, side, side,
    )


def per_device(pressure_source, solid_temp, gas_wall_temp, phase_map, phase_conductivity):
    groups = lax.axis_size("grp")
    pencils = lax.axis_size("pen")
    group_idx = lax.axis_index("grp")
    pencil_idx = lax.axis_index("pen")
    depth_loc, span_len, stream_loc = pressure_source.shape
    stream_len = stream_loc * pencils
    depth_len = depth_loc * groups
    half = span_len // 2
    waves_loc = span_len // groups
    steps = stream_loc // SEGMENTS
    f32 = jnp.float32

    order = wave_order(span_len, groups)
    row = np.arange(half)
    table = np.stack([cas(row[:, None] * (2 * row + parity)[None, :], span_len) for parity in (0, 1)])
    table_high = table.astype(jnp.bfloat16)
    table_low = (table - table_high.astype(np.float64)).astype(jnp.bfloat16)
    table_parts = jnp.asarray(np.stack([table_high, table_low], axis=1))
    lambdas, vectors = depth_modes(depth_len)
    eigen_span = 2.0 * np.cos(2.0 * math.pi * order / span_len) - 2.0
    shift = lambdas[None, :, None] - eigen_span[:, None, :]
    root = 2.0 / (shift + 2.0 + np.sqrt(shift * (shift + 4.0)))
    gain = -1.0 / (1.0 / root - root) / span_len
    around = np.arange(pencils)[:, None, None, None]
    reach = np.power(root, stream_loc * around) / (1.0 - np.power(root, stream_len))

    def mine(constant, axis):
        chosen = lax.dynamic_index_in_dim(jnp.asarray(constant, f32), group_idx, axis, keepdims=False)
        return chosen

    root_loc = mine(root, 0)
    gain_loc = mine(gain, 0)
    hop_loc = mine(np.power(root, steps), 0)
    reach_loc = mine(reach, 1)
    falling = jnp.roll(jnp.flip(reach_loc, 0), 1, 0)
    reach_left = lax.dynamic_slice_in_dim(
        jnp.concatenate([falling, falling]), (pencils + 1 - pencil_idx) % pencils, pencils, 0
    )
    reach_right = lax.dynamic_slice_in_dim(
        jnp.concatenate([reach_loc, reach_loc]), (2 * pencils - 1 - pencil_idx) % pencils, pencils, 0
    )

    tile_rows = span_len // groups

    def conductivity(phases):
        return jnp.where(phases == 1, phase_conductivity[1], phase_conductivity[0])

    solid_len = solid_temp.shape[0]
    edge_rows = [
        jnp.concatenate([solid_temp[:, part], conductivity(phase_map[:, part]), gas_wall_temp[None, part]])
        for part in (slice(0, ROWS), slice(tile_rows - ROWS, tile_rows))
    ]
    above, below = swap_edges(jnp.concatenate(edge_rows, axis=1), "grp", 1, ROWS)
    spectral = pl.pallas_call(
        span_forward_kernel,
        grid=(depth_loc,),
        in_specs=[
            pl.BlockSpec((1, span_len, stream_loc), lambda z: (z, 0, 0)),
            pl.BlockSpec((2, 2, half, half), lambda z: (0, 0, 0, 0)),
        ],
        out_specs=pl.BlockSpec((groups, 1, stream_loc, waves_loc), lambda z: (0, z, 0, 0)),
        out_shape=jax.ShapeDtypeStruct((groups, depth_loc, stream_loc, waves_loc), f32),
        compiler_params=params(),
        cost_estimate=pl.CostEstimate(
            flops=6 * depth_loc * stream_loc * span_len * half,
            bytes_accessed=8 * depth_loc * stream_loc * span_len,
            transcendentals=0,
        ),
        name="span_forward",
    )(pressure_source, table_parts)
    spectral, above, below = lax.optimization_barrier((spectral, above, below))
    moved = lax.all_to_all(spectral, "grp", split_axis=0, concat_axis=0, tiled=True)
    edge_cols = []
    for part in (slice(0, WIDTH), slice(stream_loc - WIDTH, stream_loc)):
        inner = jnp.concatenate(
            [solid_temp[:, :, part], conductivity(phase_map[:, :, part]), gas_wall_temp[None, :, part]]
        )
        edge_cols.append(jnp.concatenate([above[:, :, part], inner, below[:, :, part]], axis=1))
    before, after = swap_edges(jnp.concatenate(edge_cols, axis=2), "pen", 2, WIDTH)
    gap = jnp.zeros(before.shape[:2] + (LANES - 2 * WIDTH,), f32)
    side = jnp.concatenate([after, gap, before], axis=2)
    moved, side = lax.optimization_barrier((moved, side))
    unheated = two_steps(
        solid_temp, phase_map, phase_conductivity, above, below, side
    )

    def top_plane(inner, plane):
        rows = jnp.concatenate([above[plane, -1:], inner, below[plane, :1]])
        span = slice(ROWS - 1, ROWS + tile_rows + 1)
        return jnp.concatenate([before[plane, span, -1:], rows, after[plane, span, :1]], axis=1)

    top_cond = top_plane(conductivity(phase_map[0]), solid_len)
    dry_flux = top_plane(gas_wall_temp, 2 * solid_len) - top_plane(solid_temp[0], 0)
    moved = moved.reshape(depth_len, stream_loc, waves_loc)

    data_spec = pl.BlockSpec((depth_len, stream_loc, LANES), lambda w: (0, 0, w))
    mode_spec = pl.BlockSpec((depth_len, steps, SEGMENTS, LANES), lambda w: (0, 0, 0, w))
    wave_spec = pl.BlockSpec((depth_len, 1, LANES), lambda w: (0, 0, w))
    ends_spec = pl.BlockSpec((depth_len, SEGMENTS, LANES), lambda w: (0, 0, w))
    ends_shape = jax.ShapeDtypeStruct((depth_len, SEGMENTS, waves_loc), f32)
    cost = pl.CostEstimate(
        flops=2 * depth_len**2 * stream_loc * waves_loc,
        bytes_accessed=8 * depth_len * stream_loc * waves_loc,
        transcendentals=0,
    )

    def rowed(value):
        return value[:, None, :]

    modes, heads, tails = pl.pallas_call(
        lambda s, r, m, h, t: ends_kernel(vectors, s, FirstRow(r), m, h, t),
        grid=(waves_loc // LANES,),
        in_specs=[data_spec, wave_spec],
        out_specs=[mode_spec, ends_spec, ends_spec],
        out_shape=[
            jax.ShapeDtypeStruct((depth_len, steps, SEGMENTS, waves_loc), f32),
            ends_shape,
            ends_shape,
        ],
        compiler_params=params(),
        cost_estimate=cost,
        name="stream_ends",
    )(moved, rowed(root_loc))
    tail_all = tails[:, 0]
    head_all = heads[:, SEGMENTS - 1]
    for part in range(1, SEGMENTS):
        tail_all = tails[:, part] + hop_loc * tail_all
        head_all = heads[:, SEGMENTS - 1 - part] + hop_loc * head_all
    gathered = lax.all_gather(jnp.stack([tail_all, head_all]), "pen")
    left = [jnp.sum(reach_left * gathered[:, 0], axis=0)]
    right = [jnp.sum(reach_right * gathered[:, 1], axis=0)]
    for part in range(SEGMENTS - 1):
        left.append(tails[:, part] + hop_loc * left[-1])
        right.append(heads[:, SEGMENTS - 1 - part] + hop_loc * right[-1])
    solved = pl.pallas_call(
        lambda m, r, g, a, b, o, c: solve_kernel(vectors, m, FirstRow(r), FirstRow(g), a, b, o, c),
        grid=(waves_loc // LANES,),
        in_specs=[mode_spec, wave_spec, wave_spec, ends_spec, ends_spec],
        out_specs=data_spec,
        out_shape=jax.ShapeDtypeStruct((depth_len, stream_loc, waves_loc), f32),
        scratch_shapes=[pltpu.VMEM((depth_len, steps, SEGMENTS, LANES), f32)],
        compiler_params=params(),
        cost_estimate=cost,
        name="stream_solve",
    )(modes, rowed(root_loc), rowed(gain_loc), jnp.stack(left, 1), jnp.stack(right[::-1], 1))

    returned = lax.all_to_all(
        solved.reshape(groups, depth_loc, stream_loc, waves_loc),
        "grp",
        split_axis=0,
        concat_axis=0,
        tiled=True,
    )
    pressure = pl.pallas_call(
        span_inverse_kernel,
        grid=(depth_loc,),
        in_specs=[
            pl.BlockSpec((groups, 1, stream_loc, waves_loc), lambda z: (0, z, 0, 0)),
            pl.BlockSpec((2, 2, half, half), lambda z: (0, 0, 0, 0)),
        ],
        out_specs=pl.BlockSpec((1, span_len, stream_loc), lambda z: (z, 0, 0)),
        out_shape=jax.ShapeDtypeStruct((depth_loc, span_len, stream_loc), f32),
        compiler_params=params(),
        cost_estimate=pl.CostEstimate(
            flops=6 * depth_loc * stream_loc * span_len * half,
            bytes_accessed=8 * depth_loc * stream_loc * span_len,
            transcendentals=0,
        ),
        name="span_inverse",
    )(returned, table_parts)

    span_rows = np.arange(-1, span_len + 1) % span_len
    wall_table = cas(span_rows[:, None] * order.reshape(1, -1), span_len)
    wall_rows = lax.dynamic_slice_in_dim(
        jnp.asarray(wall_table, f32), group_idx * tile_rows, tile_rows + 2, 0
    )
    wall_waves = lax.all_gather(solved[0], "grp")
    wall = jnp.einsum(
        "ygk,gxk->yx",
        wall_rows.reshape(tile_rows + 2, groups, waves_loc),
        wall_waves,
        precision=HIGH,
        preferred_element_type=f32,
    )
    wall_left, wall_right = swap_edges(wall, "pen", 1, 1)
    wall = jnp.concatenate([wall_left, wall, wall_right], axis=1)
    flux = (HEAT_TRANSFER * (dry_flux + PRESSURE_WORK * wall))[None]
    centre_flux = flux[0, 1:-1, 1:-1]
    between = 0.5 * (top_cond[1:-1, 1:-1] + conductivity(phase_map[1])) * centre_flux
    lateral = conduct(flux, top_cond[None])[0]
    top = STEP_RATE * (centre_flux + lateral - STEP_RATE * between)
    second = STEP_RATE * STEP_RATE * between
    final_temp = unheated.at[0].add(top).at[1].add(second)
    return (pressure, final_temp)


class FirstRow:
    def __init__(self, ref):
        self.ref = ref

    def __getitem__(self, mode):
        return self.ref[mode, 0]


def solution(mesh):
    in_specs = (
        P("grp", None, "pen"),
        P(None, "grp", "pen"),
        P("grp", "pen"),
        P(None, "grp", "pen"),
        P(),
    )
    out_specs = (P("grp", None, "pen"), P(None, "grp", "pen"))
    return jax.shard_map(
        per_device, mesh=mesh, in_specs=in_specs, out_specs=out_specs, check_vma=False
    )
```
